256 devices in a mesh: ctx: 32 (over x_lo, z, core), head: 8 (over y, x_hi).
Axes of the slice: x: 4 (x_hi: 2, x_lo: 2; x = x_hi * 2 + x_lo), y: 4, z: 8, core: 2. Of those that a mesh axis runs over, the one named last changes fastest.
Arguments:
- queries: bfloat16 [8192, 2048], P('ctx', 'head'), may hold values from -6 to 6
- keys: bfloat16 [8192, 2048], P('ctx', 'head'), may hold values from -6 to 6
- values: bfloat16 [8192, 2048], P('ctx', 'head'), may hold values from -12 to 12
- frame_mask: int32 [64, 64], replicated, may hold values from 0 to 1, as said below
- out_weight: bfloat16 [2048, 2048], P('head'), may hold values from -0.25 to 0.25
Outputs:
- mixed: bfloat16 [8192, 2048], P(('ctx', 'head'))
The draws below stay inside these ranges and needn't reach their ends.
Inputs may be any that keep to these rules, and one draw needn't show every extreme that they name: frame_mask[i][j] is 1 for j equal to i and 0 for j greater than i; below the diagonal each entry is 0 or 1.
All inputs are finite; a program needn't handle non-finite values.
Results may differ from the reference program's by a relative error of at most 0.017.
Values may be sent and summed in bfloat16 or wider, within the bound.
A program may use at most 64 MiB of HBM per device.

```python
import jax
import jax.numpy as jnp
from jax import lax

D = 2048
H = 16
HD = 128
FRAME_TOK = 128
NF = 64
TOKENS = 8192


def draw_queries(key, part):
    key = jax.random.fold_in(key, 12)
    field = jnp.clip(jax.random.normal(key, (TOKENS, H * HD), jnp.float32) * 1.41, -6.0, 6.0)
    return field.astype(jnp.bfloat16)


def draw_keys(key, part):
    key = jax.random.fold_in(key, 11)
    field = jnp.clip(jax.random.normal(key, (TOKENS, H * HD), jnp.float32) * 1.41, -6.0, 6.0)
    return field.astype(jnp.bfloat16)


def draw_frame_mask(key, part):
    key = jax.random.fold_in(key, 13)
    coin = jax.random.randint(key, (NF, NF), 0, 4)
    row_index = jnp.arange(NF, dtype=jnp.int32)[:, None]
    column_index = jnp.arange(NF, dtype=jnp.int32)[None, :]
    lower = jnp.where(coin > 0, 1, 0).astype(jnp.int32)
    return jnp.where(column_index == row_index, 1, jnp.where(column_index < row_index, lower, 0)).astype(jnp.int32)


def block_levels(key, extent, cuts, smallest, top_value):
    def one(dim, parts):
        steps = jax.random.uniform(jax.random.fold_in(jax.random.fold_in(key, 6), dim), (parts,), jnp.float32, smallest / len(cuts), top_value / len(cuts))
        return jnp.repeat(jnp.exp(steps), extent[dim] // parts).reshape((-1,) + (1,) * (len(extent) - dim - 1))

    gain = one(*cuts[0])
    for cut in cuts[1:]:
        gain = gain * one(*cut)
    return gain


def centred(own_key, dims, spread, most, cuts=(), kind=jnp.bfloat16):
    level = block_levels(own_key, dims, cuts, -0.22, 0.18) if cuts else 1.0
    entries = jax.random.normal(own_key, dims, jnp.float32) * spread * level
    return jnp.minimum(jnp.maximum(entries, -most), most).astype(kind)


def setup_inputs(seed: int = 0) -> dict:
    seeds = jax.random.split(jax.random.key(seed), 6)
    queries = draw_queries(jax.random.fold_in(seeds[5], 71), 0)
    keys = draw_keys(jax.random.fold_in(seeds[5], 71), 0)
    values = centred(seeds[2], (TOKENS, H * HD), 2.0, 12.0, ((0, 32), (1, 8)))
    frame_mask = draw_frame_mask(jax.random.fold_in(seeds[5], 71), 0)
    out_weight = centred(seeds[4], (H * HD, D), (H * HD // 4) ** -0.5, 0.25, ((0, 8),))
    return {"queries": queries, "keys": keys, "values": values, "frame_mask": frame_mask, "out_weight": out_weight}


def reference(queries, keys, values, frame_mask, out_weight):
    scale = HD ** -0.5
    key_float = keys.astype(jnp.float32).reshape(TOKENS, H, HD)
    value_float = values.astype(jnp.float32).reshape(TOKENS, H, HD)
    key_frames = jnp.arange(TOKENS, dtype=jnp.int32) // FRAME_TOK
    query_blocks = queries.reshape(NF, FRAME_TOK, H, HD)
    frame_ids = jnp.arange(NF, dtype=jnp.int32)

    def one_frame(inputs):
        block, frame = inputs
        allowed = jnp.take(frame_mask[frame], key_frames) > 0
        scores = jnp.einsum("qhd,khd->hqk", block.astype(jnp.float32), key_float) * scale
        scores = jnp.where(allowed[None, None, :], scores, -jnp.inf)
        top = jnp.max(scores, axis=-1, keepdims=True)
        weights = jnp.exp(scores - top)
        total = jnp.sum(weights, axis=-1)
        rounded = lax.optimization_barrier(weights.astype(jnp.bfloat16)).astype(jnp.float32)
        context = jnp.einsum("hqk,khd->qhd", rounded, value_float)
        return (context / jnp.transpose(total)[:, :, None]).astype(jnp.bfloat16)

    attended = lax.map(one_frame, (query_blocks, frame_ids)).reshape(TOKENS, H * HD)
    return jnp.dot(attended, out_weight, preferred_element_type=jnp.float32).astype(jnp.bfloat16)
```

```python
import functools
import math

import jax
import jax.numpy as jnp
from jax import lax
from jax.experimental import pallas as pl
from jax.experimental.pallas import tpu as pltpu
from jax.sharding import PartitionSpec as P

HD = 128
FRAME_TOK = 128
NZ = 8
NY = 4
NEG_FILL = -1e30
LOG2E = 1.4426950408889634
MESH = pl.DeviceIdType.MESH


def kernel(
    q_hbm, k_hbm, v_hbm, mask, w_hbm, out_ref,
    qb, kv, wb, acc, top, ob, ab, ps, pr,
    local_sem, x_send, x_recv, z_send, z_recv, d_send, d_recv,
    w_send, w_recv, o_send, o_recv, p_send, p_recv,
):
    p = lax.axis_index("ctx")
    g = lax.axis_index("head")
    core = lax.rem(p, 2)
    zc = lax.rem(p, 2 * NZ)
    z = lax.div(zc, 2)
    xl = lax.div(p, 2 * NZ)
    y = lax.div(g, 2)
    xh = lax.rem(g, 2)
    rows = q_hbm.shape[0]
    half_cols = w_hbm.shape[1] // 2

    def device(xl_, z_, core_, y_, xh_):
        return ((xl_ * NZ + z_) * 2 + core_, y_ * 2 + xh_)

    def remote(src, dst, send, recv, target):
        return pltpu.make_async_remote_copy(
            src_ref=src, dst_ref=dst, send_sem=send, recv_sem=recv,
            device_id=target, device_id_type=MESH,
        )

    z_up, z_down = lax.rem(z + 1, NZ), lax.rem(z + NZ - 1, NZ)
    y_up, y_down = lax.rem(y + 1, NY), lax.rem(y + NY - 1, NY)
    sibling = device(xl, z, 1 - core, y, xh)
    partner = device(1 - xl, z, core, y, xh)
    up = device(xl, z_up, core, y, xh)
    down = device(xl, z_down, core, y, xh)
    w_up = device(xl, z, core, y_up, xh)
    w_down = device(xl, z, core, y_down, xh)

    def group_member(i):
        h = lax.rem(xl + lax.div(i, 8), 2)
        y_ = lax.rem(y + lax.rem(lax.div(i, 2), 4), NY)
        c_ = lax.rem(core + lax.rem(i, 2), 2)
        return h, y_, device(h, z, c_, y_, xh)

    own = pl.ds(pl.multiple_of(xl * HD, HD), HD)
    other = pl.ds(pl.multiple_of((1 - xl) * HD, HD), HD)
    w_cols = pl.ds(pl.multiple_of(core * half_cols, half_cols), half_cols)
    local = [
        pltpu.make_async_copy(k_hbm.at[:, own], kv.at[xl, z, 0, core], local_sem.at[0]),
        pltpu.make_async_copy(v_hbm.at[:, own], kv.at[xl, z, 1, core], local_sem.at[1]),
        pltpu.make_async_copy(q_hbm.at[:, own], qb.at[xl], local_sem.at[2]),
        pltpu.make_async_copy(w_hbm.at[:, w_cols], wb.at[y], local_sem.at[3]),
    ]
    for copy in local:
        copy.start()

    barrier = pltpu.get_barrier_semaphore()

    def greet(i, carry):
        _, _, target = group_member(i)
        pl.semaphore_signal(barrier, inc=1, device_id=target, device_id_type=MESH)
        return carry

    for target in (
        up, down, device(xl, z, core, y, 1 - xh), device(xl, z, 1 - core, y, 1 - xh)
    ):
        pl.semaphore_signal(barrier, inc=1, device_id=target, device_id_type=MESH)
    lax.fori_loop(1, 16, greet, 0)
    pl.semaphore_wait(barrier, 19)

    exchange = [
        remote(k_hbm.at[:, other], kv.at[xl, z, 0, core], x_send.at[0], x_recv.at[0], partner),
        remote(v_hbm.at[:, other], kv.at[xl, z, 1, core], x_send.at[1], x_recv.at[1], partner),
        remote(q_hbm.at[:, other], qb.at[xl], x_send.at[2], x_recv.at[2], partner),
    ]
    for copy in exchange:
        copy.start()

    def ring(direction, h, s):
        if direction == 0:
            unit = kv.at[h, lax.rem(z + NZ - s, NZ), :, core]
            target = up
        else:
            unit = kv.at[h, lax.rem(z + s, NZ), :, core]
            target = down
        return remote(
            unit, unit, z_send.at[direction, h, s], z_recv.at[direction, h, s], target
        )

    def source(t):
        s = lax.div(t + 1, 2)
        return lax.rem(z + NZ + jnp.where(lax.rem(t, 2) == 1, -s, s), NZ)

    def share(h, t):
        unit = kv.at[h, source(t), :, core]
        return remote(unit, unit, d_send.at[h, t], d_recv.at[h, t], sibling)

    local[0].wait()
    local[1].wait()
    for direction in (0, 1):
        ring(direction, xl, 0).start()
    share(xl, 0).start()

    w_half = rows // 2
    first, second = pl.ds(0, w_half), pl.ds(w_half, w_half)

    def w_own(i):
        part = (first, second, second, first)[i]
        return remote(
            w_hbm.at[part, w_cols], wb.at[y, part], w_send.at[i], w_recv.at[i],
            (w_up, w_down, w_up, w_down)[i],
        )

    def w_forward(i):
        part = (first, second)[i]
        held = wb.at[(y_down, y_up)[i], part]
        return remote(held, held, w_send.at[4 + i], w_recv.at[4 + i], (w_up, w_down)[i])

    for i in range(4):
        w_own(i).start()

    exchange[0].wait_recv()
    exchange[1].wait_recv()
    for direction in (0, 1):
        ring(direction, 1 - xl, 0).start()
    share(1 - xl, 0).start()

    acc[...] = jnp.zeros_like(acc)
    top[...] = jnp.full(top.shape, NEG_FILL, jnp.float32)
    local[2].wait()
    exchange[2].wait_recv()

    scale = LOG2E / math.sqrt(HD)
    ones = jnp.ones((2 * rows, HD), jnp.bfloat16)

    def attend(h, src):
        q = qb[h]
        tiles = []
        for half in range(2):
            k = kv[half, src, 0].reshape(2 * rows, HD)
            s = lax.dot_general(
                q, k, (((1,), (1,)), ((), ())), preferred_element_type=jnp.float32
            )
            for j in range(2 * rows // FRAME_TOK):
                key_frame = half * 4 * NZ + src * 4 + j
                fill = []
                for f in range(rows // FRAME_TOK):
                    allowed = mask[h * 4 * NZ + zc * 2 + f, key_frame]
                    fill.append(
                        jnp.full(
                            (FRAME_TOK, FRAME_TOK),
                            jnp.where(allowed > 0, 0.0, NEG_FILL),
                            jnp.float32,
                        )
                    )
                tiles.append(
                    s[:, j * FRAME_TOK:(j + 1) * FRAME_TOK] + jnp.concatenate(fill, axis=0)
                )
        best = functools.reduce(jnp.maximum, tiles)
        old_top = top[h]
        new_top = jnp.maximum(old_top, jnp.max(best, axis=1, keepdims=True))
        weights = [jnp.exp2((tile - new_top) * scale).astype(jnp.bfloat16) for tile in tiles]
        fade = jnp.exp2((old_top - new_top) * scale)
        total = acc[h] * jnp.concatenate([fade, fade], axis=1)
        per = len(weights) // 2
        for half in range(2):
            v = kv[half, src, 1].reshape(2 * rows, HD)
            total += jnp.dot(
                jnp.concatenate(weights[half * per:(half + 1) * per], axis=1),
                jnp.concatenate([v, ones], axis=1),
                preferred_element_type=jnp.float32,
            )
        acc[h] = total
        top[h] = new_top

    def step(t, carry):
        s = lax.div(t + 1, 2)
        odd = lax.rem(t, 2) == 1

        @pl.when(odd & (t < 7))
        def _():
            for h in (xl, 1 - xl):
                ring(0, h, s - 1).wait_recv()

                @pl.when((h == 0) | (s < 3))
                def _():
                    ring(0, h, s).start()

                share(h, t).start()
                ring(1, h, s - 1).wait_recv()

                @pl.when((h == 1) | (s < 3))
                def _():
                    ring(1, h, s).start()

                share(h, t + 1).start()

        @pl.when(t == 3)
        def _():
            for i in range(2):
                w_own(i).wait_recv()
                w_forward(i).start()

        @pl.when(t == 7)
        def _():
            ring(0, 0, 3).wait_recv()
            share(0, 7).start()
            ring(1, 1, 3).wait_recv()
            share(1, 7).start()

        src = source(t)
        share(0, t).wait_recv()
        share(1, t).wait_recv()
        attend(0, src)
        attend(1, src)
        return carry

    lax.fori_loop(0, NZ, step, 0)

    for h in range(2):
        done = (acc[h, :, :HD] / acc[h, :, HD:]).astype(jnp.bfloat16)
        ob[h] = done.reshape(NY, rows // NY, HD)

    def pass_on(i):
        h, y_, target = group_member(i)
        return remote(
            ob.at[h, y_], ab.at[core, y, xl], o_send.at[i], o_recv.at[i], target
        )

    def start_pass(i, carry):
        pass_on(i).start()
        return carry

    def end_pass(i, carry):
        pass_on(i).wait_recv()
        return carry

    lax.fori_loop(1, 16, start_pass, 0)
    ab[core, y, xl] = ob[xl, y]

    for copy in exchange:
        copy.wait_send()
    for i in range(4):
        w_own(i).wait_send()
    for i in range(2):
        w_forward(i).wait_send()
    local[3].wait()
    w_own(2).wait_recv()
    w_own(3).wait_recv()
    w_forward(0).wait_recv()
    w_forward(1).wait_recv()

    def end_ring(s, carry):
        ring(0, 0, s).wait_send()
        ring(1, 1, s).wait_send()

        @pl.when(s < 3)
        def _():
            ring(0, 1, s).wait_send()
            ring(1, 0, s).wait_send()

        return carry

    def end_share(t, carry):
        share(0, t).wait_send()
        share(1, t).wait_send()
        return carry

    lax.fori_loop(0, 4, end_ring, 0)
    lax.fori_loop(0, NZ, end_share, 0)
    lax.fori_loop(1, 16, end_pass, 0)

    group_rows = 2 * (rows // NY)
    attended = jnp.concatenate(
        [ab[:, i, j].reshape(group_rows, HD) for i in range(NY) for j in range(2)], axis=1
    )
    block = 256
    for n in range(half_cols // block):
        w = wb[:, :, n * block:(n + 1) * block].reshape(NY * rows, block)
        part = jnp.dot(attended, w, preferred_element_type=jnp.float32)
        ps[:, :, :, n * block:(n + 1) * block] = part.astype(jnp.bfloat16).reshape(
            2, 2, group_rows // 4, block
        )

    def hand_over(i):
        c_ = (1 - core, core, 1 - core)[i]
        x_ = (xh, 1 - xh, 1 - xh)[i]
        return remote(
            ps.at[c_, x_], pr.at[xh, core], p_send.at[i], p_recv.at[i],
            device(xl, z, c_, y, x_),
        )

    for i in range(3):
        hand_over(i).start()
    pr[xh, core] = ps[core, xh]

    def end_send(i, carry):
        pass_on(i).wait_send()
        return carry

    lax.fori_loop(1, 16, end_send, 0)
    for i in range(3):
        hand_over(i).wait_recv()
    for c_ in range(2):
        out_ref[:, c_ * half_cols:(c_ + 1) * half_cols] = (
            pr[0, c_].astype(jnp.float32) + pr[1, c_].astype(jnp.float32)
        ).astype(out_ref.dtype)
    for i in range(3):
        hand_over(i).wait_send()


def on_device(queries, keys, values, frame_mask, out_weight):
    rows = queries.shape[0]
    width = out_weight.shape[1]
    half_cols = width // 2
    out_rows = rows // (2 * NY)
    any_spec = pl.BlockSpec(memory_space=pl.ANY)
    dma = pltpu.SemaphoreType.DMA
    bf16, f32 = jnp.bfloat16, jnp.float32
    return pl.pallas_call(
        kernel,
        out_shape=jax.ShapeDtypeStruct((out_rows, width), bf16),
        in_specs=[
            any_spec, any_spec, any_spec,
            pl.BlockSpec(memory_space=pltpu.SMEM),
            any_spec,
        ],
        out_specs=pl.BlockSpec(memory_space=pltpu.VMEM),
        scratch_shapes=[
            pltpu.VMEM((2, rows, HD), bf16),
            pltpu.VMEM((2, NZ, 2, 2, rows, HD), bf16),
            pltpu.VMEM((NY, rows, half_cols), bf16),
            pltpu.VMEM((2, rows, 2 * HD), f32),
            pltpu.VMEM((2, rows, HD), f32),
            pltpu.VMEM((2, NY, rows // NY, HD), bf16),
            pltpu.VMEM((2, NY, 2, rows // NY, HD), bf16),
            pltpu.VMEM((2, 2, out_rows, half_cols), bf16),
            pltpu.VMEM((2, 2, out_rows, half_cols), bf16),
            dma((4,)),
            dma((3,)), dma((3,)),
            dma((2, 2, 4)), dma((2, 2, 4)),
            dma((2, NZ)), dma((2, NZ)),
            dma((6,)), dma((6,)),
            dma((16,)), dma((16,)),
            dma((3,)), dma((3,)),
        ],
        compiler_params=pltpu.CompilerParams(
            collective_id=0, has_side_effects=True, vmem_limit_bytes=40 * 1024 * 1024
        ),
        cost_estimate=pl.CostEstimate(
            flops=3 * 10**9, bytes_accessed=10 * 2**20, transcendentals=4 * 2**20
        ),
    )(queries, keys, values, frame_mask, out_weight)


def solution(mesh):
    return jax.shard_map(
        on_device,
        mesh=mesh,
        in_specs=(P("ctx", "head"), P("ctx", "head"), P("ctx", "head"), P(), P("head", None)),
        out_specs=P(("ctx", "head"), None),
        check_vma=False,
    )
```

```python
import functools
import math

import jax
import jax.numpy as jnp
from jax import lax
from jax.experimental import pallas as pl
from jax.experimental.pallas import tpu as pltpu
from jax.sharding import PartitionSpec as P

HD = 128
FRAME_TOK = 128
NZ = 8
NY = 4
NEG_FILL = -1e30
LOG2E = 1.4426950408889634
MESH = pl.DeviceIdType.MESH


def kernel(
    q_hbm, k_hbm, v_hbm, mask_hbm, w_hbm, out_ref,
    mask, qb, kv, wb, acc, top, ob, ab, pf, ps, pr,
    local_sem, x_send, x_recv, z_send, z_recv, d_send, d_recv,
    w_send, w_recv, c_send, c_recv, o_send, o_recv, p_send, p_recv,
):
    p = lax.axis_index("ctx")
    g = lax.axis_index("head")
    core = lax.rem(p, 2)
    zc = lax.rem(p, 2 * NZ)
    z = lax.div(zc, 2)
    xl = lax.div(p, 2 * NZ)
    y = lax.div(g, 2)
    xh = lax.rem(g, 2)
    rows = q_hbm.shape[0]
    half_cols = w_hbm.shape[1] // 2

    def device(xl_, z_, core_, y_, xh_):
        return ((xl_ * NZ + z_) * 2 + core_, y_ * 2 + xh_)

    def remote(src, dst, send, recv, target):
        return pltpu.make_async_remote_copy(
            src_ref=src, dst_ref=dst, send_sem=send, recv_sem=recv,
            device_id=target, device_id_type=MESH,
        )

    z_up, z_down = lax.rem(z + 1, NZ), lax.rem(z + NZ - 1, NZ)
    y_up, y_down = lax.rem(y + 1, NY), lax.rem(y + NY - 1, NY)
    sibling = device(xl, z, 1 - core, y, xh)
    partner = device(1 - xl, z, core, y, xh)
    up = device(xl, z_up, core, y, xh)
    down = device(xl, z_down, core, y, xh)
    w_up = device(xl, z, core, y_up, xh)
    w_down = device(xl, z, core, y_down, xh)

    def group_member(i):
        h = lax.rem(xl + lax.div(i, NY), 2)
        y_ = lax.rem(y + i, NY)
        return h, y_, device(h, z, core, y_, xh)

    own = pl.ds(pl.multiple_of(xl * HD, HD), HD)
    other = pl.ds(pl.multiple_of((1 - xl) * HD, HD), HD)
    w_cols = pl.ds(pl.multiple_of(core * half_cols, half_cols), half_cols)
    local = [
        pltpu.make_async_copy(k_hbm.at[:, own], kv.at[xl, z, 0, core], local_sem.at[0]),
        pltpu.make_async_copy(v_hbm.at[:, own], kv.at[xl, z, 1, core], local_sem.at[1]),
        pltpu.make_async_copy(q_hbm.at[:, own], qb.at[xl], local_sem.at[2]),
        pltpu.make_async_copy(w_hbm, wb.at[y], local_sem.at[3]),
        pltpu.make_async_copy(mask_hbm, mask, local_sem.at[4]),
    ]
    for copy in local:
        copy.start()

    barrier = pltpu.get_barrier_semaphore()

    def greet(i, carry):
        _, _, target = group_member(i)
        pl.semaphore_signal(barrier, inc=1, device_id=target, device_id_type=MESH)
        return carry

    across = device(xl, z, core, y, 1 - xh)
    for target in (up, down, sibling, across):
        pl.semaphore_signal(barrier, inc=1, device_id=target, device_id_type=MESH)
    lax.fori_loop(1, 2 * NY, greet, 0)
    pl.semaphore_wait(barrier, 11)

    exchange = [
        remote(k_hbm.at[:, other], kv.at[xl, z, 0, core], x_send.at[0], x_recv.at[0], partner),
        remote(v_hbm.at[:, other], kv.at[xl, z, 1, core], x_send.at[1], x_recv.at[1], partner),
        remote(q_hbm.at[:, other], qb.at[xl], x_send.at[2], x_recv.at[2], partner),
    ]
    for copy in exchange[:2]:
        copy.start()

    def ring(direction, h, s):
        if direction == 0:
            unit = kv.at[h, lax.rem(z + NZ - s, NZ), :, core]
            target = up
        else:
            unit = kv.at[h, lax.rem(z + s, NZ), :, core]
            target = down
        return remote(
            unit, unit, z_send.at[direction, h, s], z_recv.at[direction, h, s], target
        )

    def source(t):
        s = lax.div(t + 1, 2)
        return lax.rem(z + NZ + jnp.where(lax.rem(t, 2) == 1, -s, s), NZ)

    def share(h, t):
        unit = kv.at[h, source(t), :, core]
        return remote(unit, unit, d_send.at[h, t], d_recv.at[h, t], sibling)

    local[0].wait()
    local[1].wait()
    for direction in (0, 1):
        ring(direction, xl, 0).start()
    share(xl, 0).start()

    w_half = rows // 2
    first, second = pl.ds(0, w_half), pl.ds(w_half, w_half)

    def w_own(i):
        part = (first, second, second, first)[i]
        return remote(
            w_hbm.at[part, w_cols], wb.at[y, part, w_cols], w_send.at[i], w_recv.at[i],
            (w_up, w_down, w_up, w_down)[i],
        )

    def w_forward(i):
        part = (first, second)[i]
        held = wb.at[(y_down, y_up)[i], part, w_cols]
        return remote(held, held, w_send.at[4 + i], w_recv.at[4 + i], (w_up, w_down)[i])

    def w_share(i):
        y_far = lax.rem(y + 2, NY)
        part = (first, second, second, first, first, second)[i]
        held = wb.at[(y_down, y_up, y_down, y_up, y_far, y_far)[i], part, w_cols]
        return remote(held, held, c_send.at[i], c_recv.at[i], sibling)

    for i in range(4):
        w_own(i).start()

    exchange[0].wait_recv()
    exchange[1].wait_recv()
    exchange[2].start()
    for direction in (0, 1):
        ring(direction, 1 - xl, 0).start()
    share(1 - xl, 0).start()

    acc[...] = jnp.zeros_like(acc)
    top[...] = jnp.full(top.shape, NEG_FILL, jnp.float32)
    local[2].wait()
    local[4].wait()
    exchange[2].wait_recv()

    scale = LOG2E / math.sqrt(HD)
    ones = jnp.ones((2 * rows, HD), jnp.bfloat16)

    def attend(h, src):
        q = qb[h]
        tiles = []
        for half in range(2):
            k = kv[half, src, 0].reshape(2 * rows, HD)
            s = lax.dot_general(
                q, k, (((1,), (1,)), ((), ())), preferred_element_type=jnp.float32
            )
            for j in range(2 * rows // FRAME_TOK):
                key_frame = half * 4 * NZ + src * 4 + j
                fill = []
                for f in range(rows // FRAME_TOK):
                    allowed = mask[h * 4 * NZ + zc * 2 + f, key_frame]
                    fill.append(
                        jnp.full(
                            (FRAME_TOK, FRAME_TOK),
                            jnp.where(allowed > 0, 0.0, NEG_FILL),
                            jnp.float32,
                        )
                    )
                tiles.append(
                    s[:, j * FRAME_TOK:(j + 1) * FRAME_TOK] + jnp.concatenate(fill, axis=0)
                )
        best = functools.reduce(jnp.maximum, tiles)
        old_top = top[h]
        new_top = jnp.maximum(old_top, jnp.max(best, axis=1, keepdims=True))
        weights = [jnp.exp2((tile - new_top) * scale).astype(jnp.bfloat16) for tile in tiles]
        fade = jnp.exp2((old_top - new_top) * scale)
        total = acc[h] * jnp.concatenate([fade, fade], axis=1)
        per = len(weights) // 2
        for half in range(2):
            v = kv[half, src, 1].reshape(2 * rows, HD)
            total += jnp.dot(
                jnp.concatenate(weights[half * per:(half + 1) * per], axis=1),
                jnp.concatenate([v, ones], axis=1),
                preferred_element_type=jnp.float32,
            )
        acc[h] = total
        top[h] = new_top

    def step(t, carry):
        s = lax.div(t + 1, 2)
        odd = lax.rem(t, 2) == 1

        @pl.when(odd & (t < 7))
        def _():
            for h in (xl, 1 - xl):
                ring(0, h, s - 1).wait_recv()

                @pl.when((h == 0) | (s < 3))
                def _():
                    ring(0, h, s).start()

                share(h, t).start()
                ring(1, h, s - 1).wait_recv()

                @pl.when((h == 1) | (s < 3))
                def _():
                    ring(1, h, s).start()

                share(h, t + 1).start()

        @pl.when(t == 3)
        def _():
            for i in range(2):
                w_own(i).wait_recv()
                w_forward(i).start()
                w_share(i).start()

        @pl.when(t == 5)
        def _():
            for i in range(2, 4):
                w_own(i).wait_recv()
                w_share(i).start()

        src = source(t)
        share(0, t).wait_recv()
        share(1, t).wait_recv()
        attend(0, src)
        attend(1, src)
        return carry

    def pass_on(i):
        h, y_, target = group_member(i)
        return remote(
            ob.at[h, y_], ab.at[y, xl], o_send.at[i], o_recv.at[i], target
        )

    def end_pass(i, carry):
        pass_on(i).wait_recv()
        return carry

    lax.fori_loop(0, NZ - 1, step, 0)

    for i in range(2):
        w_forward(i).wait_recv()
        w_share(4 + i).start()
    ring(0, 0, 3).wait_recv()
    share(0, 7).start()
    ring(1, 1, 3).wait_recv()
    share(1, 7).start()
    share(0, 7).wait_recv()
    share(1, 7).wait_recv()
    for i in range(2):
        h = lax.rem(xl + 1 + i, 2)
        attend(h, source(7))
        done = (acc[h, :, :HD] / acc[h, :, HD:]).astype(jnp.bfloat16)
        ob[h] = done.reshape(NY, rows // NY, HD)
        for j in range(NY):
            if i == 0 or j > 0:
                pass_on((1 - i) * NY + j).start()
    ab[y, xl] = ob[xl, y]

    for copy in exchange:
        copy.wait_send()
    for i in range(4):
        w_own(i).wait_send()
    for i in range(2):
        w_forward(i).wait_send()
    for i in range(6):
        w_share(i).wait_send()
        w_share(i).wait_recv()
    local[3].wait()

    def end_ring(s, carry):
        ring(0, 0, s).wait_send()
        ring(1, 1, s).wait_send()

        @pl.when(s < 3)
        def _():
            ring(0, 1, s).wait_send()
            ring(1, 0, s).wait_send()

        return carry

    def end_share(t, carry):
        share(0, t).wait_send()
        share(1, t).wait_send()
        return carry

    lax.fori_loop(0, 4, end_ring, 0)
    lax.fori_loop(0, NZ, end_share, 0)
    lax.fori_loop(1, 2 * NY, end_pass, 0)

    attended = jnp.concatenate([ab[i, j] for i in range(NY) for j in range(2)], axis=1)
    out_rows, width = out_ref.shape
    block = width // 4

    def hand_over(i):
        cols = pl.ds(i * block, block)
        return remote(
            ps.at[1 - xh, :, cols], pr.at[:, cols], p_send.at[i], p_recv.at[i], across
        )

    for i in range(4):
        cols = slice(i * block, (i + 1) * block)
        part = jnp.dot(
            attended, wb[:, :, cols].reshape(NY * rows, block),
            preferred_element_type=jnp.float32,
        ).reshape(2, out_rows, block)
        pf[:, :, cols] = part
        ps[:, :, cols] = part.astype(jnp.bfloat16)
        hand_over(i).start()

    def end_send(i, carry):
        pass_on(i).wait_send()
        return carry

    lax.fori_loop(1, 2 * NY, end_send, 0)
    for i in range(4):
        cols = slice(i * block, (i + 1) * block)
        hand_over(i).wait_recv()
        out_ref[:, cols] = (
            pf[xh, :, cols] + pr[:, cols].astype(jnp.float32)
        ).astype(out_ref.dtype)
    for i in range(4):
        hand_over(i).wait_send()


def on_device(queries, keys, values, frame_mask, out_weight):
    rows = queries.shape[0]
    width = out_weight.shape[1]
    out_rows = rows // (2 * NY)
    hbm_spec = pl.BlockSpec(memory_space=pltpu.HBM)
    dma = pltpu.SemaphoreType.DMA
    bf16, f32 = jnp.bfloat16, jnp.float32
    return pl.pallas_call(
        kernel,
        out_shape=jax.ShapeDtypeStruct((out_rows, width), bf16),
        in_specs=[hbm_spec] * 5,
        out_specs=pl.BlockSpec(memory_space=pltpu.VMEM),
        scratch_shapes=[
            pltpu.SMEM(frame_mask.shape, frame_mask.dtype),
            pltpu.VMEM((2, rows, HD), bf16),
            pltpu.VMEM((2, NZ, 2, 2, rows, HD), bf16),
            pltpu.VMEM((NY, rows, width), bf16),
            pltpu.VMEM((2, rows, 2 * HD), f32),
            pltpu.VMEM((2, rows, HD), f32),
            pltpu.VMEM((2, NY, rows // NY, HD), bf16),
            pltpu.VMEM((NY, 2, rows // NY, HD), bf16),
            pltpu.VMEM((2, out_rows, width), f32),
            pltpu.VMEM((2, out_rows, width), bf16),
            pltpu.VMEM((out_rows, width), bf16),
            dma((5,)),
            dma((3,)), dma((3,)),
            dma((2, 2, 4)), dma((2, 2, 4)),
            dma((2, NZ)), dma((2, NZ)),
            dma((6,)), dma((6,)),
            dma((6,)), dma((6,)),
            dma((2 * NY,)), dma((2 * NY,)),
            dma((4,)), dma((4,)),
        ],
        compiler_params=pltpu.CompilerParams(
            collective_id=0, has_side_effects=True, vmem_limit_bytes=55040 * 1024
        ),
        cost_estimate=pl.CostEstimate(
            flops=3 * 10**9, bytes_accessed=10 * 2**20, transcendentals=4 * 2**20
        ),
    )(queries, keys, values, frame_mask, out_weight)


def solution(mesh):
    return jax.shard_map(
        on_device,
        mesh=mesh,
        in_specs=(P("ctx", "head"), P("ctx", "head"), P("ctx", "head"), P(), P("head", None)),
        out_specs=P(("ctx", "head"), None),
        check_vma=False,
    )
```

```python
import functools
import math

import jax
import jax.numpy as jnp
from jax import lax
from jax.experimental import pallas as pl
from jax.experimental.pallas import tpu as pltpu
from jax.sharding import PartitionSpec as P

HD = 128
FRAME_TOK = 128
NZ = 8
NY = 4
NEG_FILL = -1e30
LOG2E = 1.4426950408889634
MESH = pl.DeviceIdType.MESH


def kernel(
    q_hbm, k_hbm, v_hbm, mask_hbm, w_hbm, out_ref,
    mask, qb, kv, wb, acc, top, ob, ab, pf, ps, pr,
    local_sem, x_send, x_recv, z_send, z_recv, d_send, d_recv, e_send, e_recv,
    w_send, w_recv, c_send, c_recv, o_send, o_recv, p_send, p_recv,
):
    p = lax.axis_index("ctx")
    g = lax.axis_index("head")
    core = lax.rem(p, 2)
    zc = lax.rem(p, 2 * NZ)
    z = lax.div(zc, 2)
    xl = lax.div(p, 2 * NZ)
    y = lax.div(g, 2)
    xh = lax.rem(g, 2)
    rows = q_hbm.shape[0]
    half_cols = w_hbm.shape[1] // 2

    def device(xl_, z_, core_, y_, xh_):
        return ((xl_ * NZ + z_) * 2 + core_, y_ * 2 + xh_)

    def remote(src, dst, send, recv, target):
        return pltpu.make_async_remote_copy(
            src_ref=src, dst_ref=dst, send_sem=send, recv_sem=recv,
            device_id=target, device_id_type=MESH,
        )

    z_up, z_down = lax.rem(z + 1, NZ), lax.rem(z + NZ - 1, NZ)
    y_up, y_down = lax.rem(y + 1, NY), lax.rem(y + NY - 1, NY)
    sibling = device(xl, z, 1 - core, y, xh)
    partner = device(1 - xl, z, core, y, xh)
    up = device(xl, z_up, core, y, xh)
    down = device(xl, z_down, core, y, xh)
    w_up = device(xl, z, core, y_up, xh)
    w_down = device(xl, z, core, y_down, xh)

    def group_member(i):
        h = lax.rem(xl + lax.div(i, NY), 2)
        y_ = lax.rem(y + i, NY)
        return h, y_, device(h, z, core, y_, xh)

    own = pl.ds(pl.multiple_of(xl * HD, HD), HD)
    other = pl.ds(pl.multiple_of((1 - xl) * HD, HD), HD)
    w_cols = pl.ds(pl.multiple_of(core * half_cols, half_cols), half_cols)
    local = [
        pltpu.make_async_copy(k_hbm.at[:, own], kv.at[xl, z, core, 0], local_sem.at[0]),
        pltpu.make_async_copy(v_hbm.at[:, own], kv.at[xl, z, core, 1], local_sem.at[1]),
        pltpu.make_async_copy(q_hbm.at[:, own], qb.at[xl], local_sem.at[2]),
        pltpu.make_async_copy(w_hbm, wb.at[y], local_sem.at[3]),
        pltpu.make_async_copy(mask_hbm, mask, local_sem.at[4]),
    ]
    for copy in local:
        copy.start()

    barrier = pltpu.get_barrier_semaphore()

    def greet(i, carry):
        _, _, target = group_member(i)
        pl.semaphore_signal(barrier, inc=1, device_id=target, device_id_type=MESH)
        return carry

    across = device(xl, z, core, y, 1 - xh)
    for target in (up, down, sibling, across):
        pl.semaphore_signal(barrier, inc=1, device_id=target, device_id_type=MESH)
    lax.fori_loop(1, 2 * NY, greet, 0)
    pl.semaphore_wait(barrier, 11)

    exchange = [
        remote(k_hbm.at[:, other], kv.at[xl, z, core, 0], x_send.at[0], x_recv.at[0], partner),
        remote(v_hbm.at[:, other], kv.at[xl, z, core, 1], x_send.at[1], x_recv.at[1], partner),
        remote(q_hbm.at[:, other], qb.at[xl], x_send.at[2], x_recv.at[2], partner),
    ]
    for copy in exchange[:2]:
        copy.start()

    def ring(direction, h, s):
        if direction == 0:
            unit = kv.at[h, lax.rem(z + NZ - s, NZ), core]
            target = up
        else:
            unit = kv.at[h, lax.rem(z + s, NZ), core]
            target = down
        return remote(
            unit, unit, z_send.at[direction, h, s], z_recv.at[direction, h, s], target
        )

    def ring_end(direction, h):
        piece = kv.at[h, lax.rem(z + (NZ - 3, 3)[direction], NZ), core, direction]
        return remote(
            piece, piece, z_send.at[direction, h, 3], z_recv.at[direction, h, 3],
            (up, down)[direction],
        )

    def share_end(kind, h):
        piece = kv.at[h, source(NZ - 1), core, kind]
        return remote(piece, piece, e_send.at[kind, h], e_recv.at[kind, h], sibling)

    def source(t):
        s = lax.div(t + 1, 2)
        return lax.rem(z + NZ + jnp.where(lax.rem(t, 2) == 1, -s, s), NZ)

    def share(h, t):
        unit = kv.at[h, source(t), core]
        return remote(unit, unit, d_send.at[h, t], d_recv.at[h, t], sibling)

    local[0].wait()
    local[1].wait()
    for direction in (0, 1):
        ring(direction, xl, 0).start()
    share(xl, 0).start()

    w_half = rows // 2
    first, second = pl.ds(0, w_half), pl.ds(w_half, w_half)

    def w_own(i):
        part = (first, second, second, first)[i]
        return remote(
            w_hbm.at[part, w_cols], wb.at[y, part, w_cols], w_send.at[i], w_recv.at[i],
            (w_up, w_down, w_up, w_down)[i],
        )

    def w_forward(i):
        part = (first, second)[i]
        held = wb.at[(y_down, y_up)[i], part, w_cols]
        return remote(held, held, w_send.at[4 + i], w_recv.at[4 + i], (w_up, w_down)[i])

    def w_share(i):
        y_far = lax.rem(y + 2, NY)
        part = (first, second, second, first, first, second)[i]
        held = wb.at[(y_down, y_up, y_down, y_up, y_far, y_far)[i], part, w_cols]
        return remote(held, held, c_send.at[i], c_recv.at[i], sibling)

    for i in range(4):
        w_own(i).start()

    exchange[0].wait_recv()
    exchange[1].wait_recv()
    exchange[2].start()
    for direction in (0, 1):
        ring(direction, 1 - xl, 0).start()
    share(1 - xl, 0).start()

    acc[...] = jnp.zeros_like(acc)
    top[...] = jnp.full(top.shape, NEG_FILL, jnp.float32)

    scale = LOG2E / math.sqrt(HD)
    ones = jnp.ones((2 * rows, HD), jnp.bfloat16)

    def scores(q, half, src):
        k = kv[half, src, :, 0].reshape(2 * rows, HD)
        return lax.dot_general(
            q, k, (((1,), (1,)), ((), ())), preferred_element_type=jnp.float32
        )

    def absorb(h, parts):
        tiles = []
        for half, src in parts:
            s = scores(qb[h], half, src)
            for j in range(2 * rows // FRAME_TOK):
                key_frame = half * 4 * NZ + src * 4 + j
                fill = []
                for f in range(rows // FRAME_TOK):
                    allowed = mask[h * 4 * NZ + zc * 2 + f, key_frame]
                    fill.append(
                        jnp.full(
                            (FRAME_TOK, FRAME_TOK),
                            jnp.where(allowed > 0, 0.0, NEG_FILL),
                            jnp.float32,
                        )
                    )
                tiles.append(
                    s[:, j * FRAME_TOK:(j + 1) * FRAME_TOK] + jnp.concatenate(fill, axis=0)
                )
        best = functools.reduce(jnp.maximum, tiles)
        old_top = top[h]
        new_top = jnp.maximum(old_top, jnp.max(best, axis=1, keepdims=True))
        weights = [jnp.exp2((tile - new_top) * scale).astype(jnp.bfloat16) for tile in tiles]
        fade = jnp.exp2((old_top - new_top) * scale)
        total = acc[h] * jnp.concatenate([fade, fade], axis=1)
        per = 2 * rows // FRAME_TOK
        for i, (half, src) in enumerate(parts):
            v = kv[half, src, :, 1].reshape(2 * rows, HD)
            total += jnp.dot(
                jnp.concatenate(weights[i * per:(i + 1) * per], axis=1),
                jnp.concatenate([v, ones], axis=1),
                preferred_element_type=jnp.float32,
            )
        acc[h] = total
        top[h] = new_top

    def attend(*sources):
        absorb(0, [(0, src) for src in sources])
        absorb(1, [(half, src) for src in sources for half in (0, 1)])

    def step(u, carry):
        s, h = lax.div(u, 2) + 1, lax.rem(xl + u, 2)

        @pl.when(s < 4)
        def _():
            for direction in (0, 1):
                ring(direction, h, s - 1).wait_recv()

                @pl.when(s < 3)
                def _():
                    ring(direction, h, s).start()

                @pl.when(s == 3)
                def _():
                    ring_end(direction, h).start()

                share(h, 2 * s - 1 + direction).start()

        @pl.when(s == 4)
        def _():
            for direction in (0, 1):
                ring_end(direction, h).wait_recv()
                share_end(direction, h).start()

        @pl.when(u == 1)
        def _():
            local[2].wait()
            local[4].wait()
            exchange[2].wait_recv()

        @pl.when(u == 3)
        def _():
            for i in range(2):
                w_own(i).wait_recv()
                w_forward(i).start()
                w_share(i).start()

        @pl.when(u == 5)
        def _():
            for i in range(2, 4):
                w_own(i).wait_recv()
                w_share(i).start()

        @pl.when((u > 0) & (u < NZ))
        def _():
            for h_ in (0, 1):
                share(h_, u - 1).wait_recv()

        @pl.when(u == NZ)
        def _():
            for h_ in (0, 1):
                for kind in (0, 1):
                    share_end(kind, h_).wait_recv()

        @pl.when(u > 0)
        def _():
            attend(source(u - 1))

        return carry

    def pass_on(i):
        h, y_, target = group_member(i)
        return remote(
            ob.at[h, y_], ab.at[y, xl], o_send.at[i], o_recv.at[i], target
        )

    def end_pass(i, carry):
        pass_on(i).wait_recv()
        return carry

    lax.fori_loop(0, NZ + 1, step, 0)
    def conclude(i, carry):
        h = lax.rem(xl + 1 + i, 2)
        done = (acc[h, :, :HD] / acc[h, :, HD:]).astype(jnp.bfloat16)
        ob[h] = done.reshape(NY, rows // NY, HD)

        def start_pass(j, carry):
            pass_on((1 - i) * NY + j).start()
            return carry

        lax.fori_loop(i, NY, start_pass, 0)
        return carry

    lax.fori_loop(0, 2, conclude, 0)
    ab[y, xl] = ob[xl, y]

    for i in range(2):
        w_forward(i).wait_recv()
        w_share(4 + i).start()

    for copy in exchange:
        copy.wait_send()
    for i in range(4):
        w_own(i).wait_send()
    for i in range(2):
        w_forward(i).wait_send()
    for i in range(6):
        w_share(i).wait_send()
        w_share(i).wait_recv()
    local[3].wait()

    def end_ring(s, carry):
        for direction in (0, 1):
            for h in (0, 1):
                ring(direction, h, s).wait_send()
        return carry

    def end_share(t, carry):
        share(0, t).wait_send()
        share(1, t).wait_send()
        return carry

    lax.fori_loop(0, 3, end_ring, 0)
    lax.fori_loop(0, NZ - 1, end_share, 0)
    for direction in (0, 1):
        for h in (0, 1):
            ring_end(direction, h).wait_send()
            share_end(direction, h).wait_send()
    lax.fori_loop(1, 2 * NY, end_pass, 0)

    attended = jnp.concatenate([ab[i, j] for i in range(NY) for j in range(2)], axis=1)
    out_rows, width = out_ref.shape
    block = width // 4

    def hand_over(i):
        cols = pl.ds(pl.multiple_of(i * block, block), block)
        return remote(
            ps.at[1 - xh, :, cols], pr.at[:, cols], p_send.at[i], p_recv.at[i], across
        )

    def project(i, carry):
        cols = pl.ds(pl.multiple_of(i * block, block), block)
        part = jnp.dot(
            attended, wb[:, :, cols].reshape(NY * rows, block),
            preferred_element_type=jnp.float32,
        ).reshape(2, out_rows, block)
        pf[:, :, cols] = part
        ps[:, :, cols] = part.astype(jnp.bfloat16)
        hand_over(i).start()
        return carry

    lax.fori_loop(0, 4, project, 0)

    def end_send(i, carry):
        pass_on(i).wait_send()
        return carry

    lax.fori_loop(1, 2 * NY, end_send, 0)
    def finish(i, carry):
        cols = pl.ds(pl.multiple_of(i * block, block), block)
        hand_over(i).wait_recv()
        out_ref[:, cols] = (
            pf[xh, :, cols] + pr[:, cols].astype(jnp.float32)
        ).astype(out_ref.dtype)
        return carry

    lax.fori_loop(0, 4, finish, 0)
    for i in range(4):
        hand_over(i).wait_send()


def on_device(queries, keys, values, frame_mask, out_weight):
    rows = queries.shape[0]
    width = out_weight.shape[1]
    out_rows = rows // (2 * NY)
    hbm_spec = pl.BlockSpec(memory_space=pltpu.HBM)
    dma = pltpu.SemaphoreType.DMA
    bf16, f32 = jnp.bfloat16, jnp.float32
    return pl.pallas_call(
        kernel,
        out_shape=jax.ShapeDtypeStruct((out_rows, width), bf16),
        in_specs=[hbm_spec] * 5,
        out_specs=pl.BlockSpec(memory_space=pltpu.VMEM),
        scratch_shapes=[
            pltpu.SMEM(frame_mask.shape, frame_mask.dtype),
            pltpu.VMEM((2, rows, HD), bf16),
            pltpu.VMEM((2, NZ, 2, 2, rows, HD), bf16),
            pltpu.VMEM((NY, rows, width), bf16),
            pltpu.VMEM((2, rows, 2 * HD), f32),
            pltpu.VMEM((2, rows, HD), f32),
            pltpu.VMEM((2, NY, rows // NY, HD), bf16),
            pltpu.VMEM((NY, 2, rows // NY, HD), bf16),
            pltpu.VMEM((2, out_rows, width), f32),
            pltpu.VMEM((2, out_rows, width), bf16),
            pltpu.VMEM((out_rows, width), bf16),
            dma((5,)),
            dma((3,)), dma((3,)),
            dma((2, 2, 4)), dma((2, 2, 4)),
            dma((2, NZ)), dma((2, NZ)),
            dma((2, 2)), dma((2, 2)),
            dma((6,)), dma((6,)),
            dma((6,)), dma((6,)),
            dma((2 * NY,)), dma((2 * NY,)),
            dma((4,)), dma((4,)),
        ],
        compiler_params=pltpu.CompilerParams(
            collective_id=0, has_side_effects=True, vmem_limit_bytes=55040 * 1024
        ),
        cost_estimate=pl.CostEstimate(
            flops=3 * 10**9, bytes_accessed=10 * 2**20, transcendentals=4 * 2**20
        ),
    )(queries, keys, values, frame_mask, out_weight)


def solution(mesh):
    return jax.shard_map(
        on_device,
        mesh=mesh,
        in_specs=(P("ctx", "head"), P("ctx", "head"), P("ctx", "head"), P(), P("head", None)),
        out_specs=P(("ctx", "head"), None),
        check_vma=False,
    )
```

```python
import functools
import math

import jax
import jax.numpy as jnp
from jax import lax
from jax.experimental import pallas as pl
from jax.experimental.pallas import tpu as pltpu
from jax.sharding import PartitionSpec as P

HD = 128
FRAME_TOK = 128
NZ = 8
NY = 4
NEG_FILL = -1e30
LOG2E = 1.4426950408889634
MESH = pl.DeviceIdType.MESH


def kernel(
    q_hbm, k_hbm, v_hbm, mask_hbm, w_hbm, out_ref,
    mask, qb, kv, wb, acc, top, ob, ab, pf, ps, pr,
    local_sem, x_send, x_recv, z_send, z_recv, d_send, d_recv, e_send, e_recv,
    w_send, w_recv, c_send, c_recv, o_send, o_recv, p_send, p_recv,
):
    p = lax.axis_index("ctx")
    g = lax.axis_index("head")
    core = lax.rem(p, 2)
    zc = lax.rem(p, 2 * NZ)
    z = lax.div(zc, 2)
    xl = lax.div(p, 2 * NZ)
    y = lax.div(g, 2)
    xh = lax.rem(g, 2)
    rows = q_hbm.shape[0]
    half_cols = w_hbm.shape[1] // 2

    def device(xl_, z_, core_, y_, xh_):
        return ((xl_ * NZ + z_) * 2 + core_, y_ * 2 + xh_)

    def remote(src, dst, send, recv, target):
        return pltpu.make_async_remote_copy(
            src_ref=src, dst_ref=dst, send_sem=send, recv_sem=recv,
            device_id=target, device_id_type=MESH,
        )

    z_up, z_down = lax.rem(z + 1, NZ), lax.rem(z + NZ - 1, NZ)
    y_up, y_down = lax.rem(y + 1, NY), lax.rem(y + NY - 1, NY)
    sibling = device(xl, z, 1 - core, y, xh)
    partner = device(1 - xl, z, core, y, xh)
    up = device(xl, z_up, core, y, xh)
    down = device(xl, z_down, core, y, xh)
    w_up = device(xl, z, core, y_up, xh)
    w_down = device(xl, z, core, y_down, xh)

    def group_member(i):
        h = lax.rem(xl + lax.div(i, NY), 2)
        y_ = lax.rem(y + i, NY)
        return h, y_, device(h, z, core, y_, xh)

    own = pl.ds(pl.multiple_of(xl * HD, HD), HD)
    other = pl.ds(pl.multiple_of((1 - xl) * HD, HD), HD)
    w_cols = pl.ds(pl.multiple_of(core * half_cols, half_cols), half_cols)
    local = [
        pltpu.make_async_copy(k_hbm.at[:, own], kv.at[xl, z, core, 0], local_sem.at[0]),
        pltpu.make_async_copy(v_hbm.at[:, own], kv.at[xl, z, core, 1], local_sem.at[1]),
        pltpu.make_async_copy(q_hbm.at[:, own], qb.at[xl], local_sem.at[2]),
        pltpu.make_async_copy(w_hbm, wb.at[y], local_sem.at[3]),
        pltpu.make_async_copy(mask_hbm, mask, local_sem.at[4]),
    ]
    for copy in local:
        copy.start()

    barrier = pltpu.get_barrier_semaphore()

    def greet(i, carry):
        _, _, target = group_member(i)
        pl.semaphore_signal(barrier, inc=1, device_id=target, device_id_type=MESH)
        return carry

    across = device(1 - xl, z, core, y, 1 - xh)
    for target in (up, down, sibling, across):
        pl.semaphore_signal(barrier, inc=1, device_id=target, device_id_type=MESH)
    lax.fori_loop(1, 2 * NY, greet, 0)
    pl.semaphore_wait(barrier, 11)

    exchange = [
        remote(k_hbm.at[:, other], kv.at[xl, z, core, 0], x_send.at[0], x_recv.at[0], partner),
        remote(v_hbm.at[:, other], kv.at[xl, z, core, 1], x_send.at[1], x_recv.at[1], partner),
        remote(q_hbm.at[:, other], qb.at[xl], x_send.at[2], x_recv.at[2], partner),
    ]
    for copy in exchange[:2]:
        copy.start()

    def ring(direction, h, s):
        if direction == 0:
            unit = kv.at[h, lax.rem(z + NZ - s, NZ), core]
            target = up
        else:
            unit = kv.at[h, lax.rem(z + s, NZ), core]
            target = down
        return remote(
            unit, unit, z_send.at[direction, h, s], z_recv.at[direction, h, s], target
        )

    def ring_end(direction, h):
        piece = kv.at[h, lax.rem(z + (NZ - 3, 3)[direction], NZ), core, direction]
        return remote(
            piece, piece, z_send.at[direction, h, 3], z_recv.at[direction, h, 3],
            (up, down)[direction],
        )

    def share_end(kind, h):
        piece = kv.at[h, source(NZ - 1), core, kind]
        return remote(piece, piece, e_send.at[kind, h], e_recv.at[kind, h], sibling)

    def source(t):
        s = lax.div(t + 1, 2)
        return lax.rem(z + NZ + jnp.where(lax.rem(t, 2) == 1, -s, s), NZ)

    def share(h, t):
        unit = kv.at[h, source(t), core]
        return remote(unit, unit, d_send.at[h, t], d_recv.at[h, t], sibling)

    local[0].wait()
    local[1].wait()
    for direction in (0, 1):
        ring(direction, xl, 0).start()
    share(xl, 0).start()

    w_half = rows // 2
    first, second = pl.ds(0, w_half), pl.ds(w_half, w_half)

    def w_own(i):
        part = (first, second, second, first)[i]
        return remote(
            w_hbm.at[part, w_cols], wb.at[y, part, w_cols], w_send.at[i], w_recv.at[i],
            (w_up, w_down, w_up, w_down)[i],
        )

    def w_forward(i):
        part = (first, second)[i]
        held = wb.at[(y_down, y_up)[i], part, w_cols]
        return remote(held, held, w_send.at[4 + i], w_recv.at[4 + i], (w_up, w_down)[i])

    def w_share(i):
        y_far = lax.rem(y + 2, NY)
        part = (first, second, second, first, first, second)[i]
        held = wb.at[(y_down, y_up, y_down, y_up, y_far, y_far)[i], part, w_cols]
        return remote(held, held, c_send.at[i], c_recv.at[i], sibling)

    for i in range(4):
        w_own(i).start()

    exchange[0].wait_recv()
    exchange[1].wait_recv()
    exchange[2].start()
    for direction in (0, 1):
        ring(direction, 1 - xl, 0).start()
    share(1 - xl, 0).start()

    acc[...] = jnp.zeros_like(acc)
    top[...] = jnp.full(top.shape, NEG_FILL, jnp.float32)

    scale = LOG2E / math.sqrt(HD)
    ones = jnp.ones((2 * rows, HD), jnp.bfloat16)

    def scores(q, half, src):
        k = kv[half, src, :, 0].reshape(2 * rows, HD)
        return lax.dot_general(
            q, k, (((1,), (1,)), ((), ())), preferred_element_type=jnp.float32
        )

    def absorb(h, parts):
        tiles = []
        for half, src in parts:
            s = scores(qb[h], half, src)
            for j in range(2 * rows // FRAME_TOK):
                key_frame = half * 4 * NZ + src * 4 + j
                fill = []
                for f in range(rows // FRAME_TOK):
                    allowed = mask[h * 4 * NZ + zc * 2 + f, key_frame]
                    fill.append(
                        jnp.full(
                            (FRAME_TOK, FRAME_TOK),
                            jnp.where(allowed > 0, 0.0, NEG_FILL),
                            jnp.float32,
                        )
                    )
                tiles.append(
                    s[:, j * FRAME_TOK:(j + 1) * FRAME_TOK] + jnp.concatenate(fill, axis=0)
                )
        best = functools.reduce(jnp.maximum, tiles)
        old_top = top[h]
        new_top = jnp.maximum(old_top, jnp.max(best, axis=1, keepdims=True))
        weights = [jnp.exp2((tile - new_top) * scale).astype(jnp.bfloat16) for tile in tiles]
        fade = jnp.exp2((old_top - new_top) * scale)
        total = acc[h] * jnp.concatenate([fade, fade], axis=1)
        per = 2 * rows // FRAME_TOK
        for i, (half, src) in enumerate(parts):
            v = kv[half, src, :, 1].reshape(2 * rows, HD)
            total += jnp.dot(
                jnp.concatenate(weights[i * per:(i + 1) * per], axis=1),
                jnp.concatenate([v, ones], axis=1),
                preferred_element_type=jnp.float32,
            )
        acc[h] = total
        top[h] = new_top

    def attend(*sources):
        absorb(0, [(0, src) for src in sources])
        absorb(1, [(half, src) for src in sources for half in (0, 1)])

    def step(u, carry):
        s, h = lax.div(u, 2) + 1, lax.rem(xl + u, 2)

        @pl.when(s < 4)
        def _():
            for direction in (0, 1):
                ring(direction, h, s - 1).wait_recv()

                @pl.when(s < 3)
                def _():
                    ring(direction, h, s).start()

                @pl.when(s == 3)
                def _():
                    ring_end(direction, h).start()

                share(h, 2 * s - 1 + direction).start()

        @pl.when(s == 4)
        def _():
            for direction in (0, 1):
                ring_end(direction, h).wait_recv()
                share_end(direction, h).start()

        @pl.when(u == 1)
        def _():
            local[2].wait()
            local[4].wait()
            exchange[2].wait_recv()

        @pl.when(u == 3)
        def _():
            for i in range(2):
                w_own(i).wait_recv()
                w_forward(i).start()
                w_share(i).start()

        @pl.when(u == 5)
        def _():
            for i in range(2, 4):
                w_own(i).wait_recv()
                w_share(i).start()

        @pl.when((u > 0) & (u < NZ))
        def _():
            for h_ in (0, 1):
                share(h_, u - 1).wait_recv()

        @pl.when(u == NZ)
        def _():
            for h_ in (0, 1):
                for kind in (0, 1):
                    share_end(kind, h_).wait_recv()

        @pl.when(u > 0)
        def _():
            attend(source(u - 1))

        return carry

    def pass_on(i):
        h, y_, target = group_member(i)
        return remote(
            ob.at[h, y_], ab.at[y, xl], o_send.at[i], o_recv.at[i], target
        )

    def end_pass(i, carry):
        pass_on(i).wait_recv()
        return carry

    lax.fori_loop(0, NZ + 1, step, 0)
    def conclude(h, carry):
        done = (acc[h, :, :HD] / acc[h, :, HD:]).astype(jnp.bfloat16).reshape(
            NY, 2, rows // (2 * NY), HD
        )
        for x_ in (0, 1):
            away = jnp.where(xh == x_, 0, 1)
            ob[jnp.where(xh == x_, h, 1 - h), :, away] = done[:, x_]
        return carry

    def start_pass(i, carry):
        pass_on(2 * NY - 1 - i).start()
        return carry

    lax.fori_loop(0, 2, conclude, 0)
    lax.fori_loop(0, 2 * NY - 1, start_pass, 0)
    ab[y, xl] = ob[xl, y]

    for i in range(2):
        w_forward(i).wait_recv()
        w_share(4 + i).start()

    for copy in exchange:
        copy.wait_send()
    for i in range(4):
        w_own(i).wait_send()
    for i in range(2):
        w_forward(i).wait_send()
    for i in range(6):
        w_share(i).wait_send()
        w_share(i).wait_recv()
    local[3].wait()

    def end_ring(s, carry):
        for direction in (0, 1):
            for h in (0, 1):
                ring(direction, h, s).wait_send()
        return carry

    def end_share(t, carry):
        share(0, t).wait_send()
        share(1, t).wait_send()
        return carry

    lax.fori_loop(0, 3, end_ring, 0)
    lax.fori_loop(0, NZ - 1, end_share, 0)
    for direction in (0, 1):
        for h in (0, 1):
            ring_end(direction, h).wait_send()
            share_end(direction, h).wait_send()
    lax.fori_loop(1, 2 * NY, end_pass, 0)

    attended = jnp.concatenate([ab[i, j].reshape(rows // NY, HD) for i in range(NY) for j in range(2)], axis=1)
    out_rows, width = out_ref.shape
    block = width // 4

    def hand_over(i):
        cols = pl.ds(pl.multiple_of(i * block, block), block)
        return remote(
            ps.at[:, cols], pr.at[:, cols], p_send.at[i], p_recv.at[i], across
        )

    def project(i, carry):
        cols = pl.ds(pl.multiple_of(i * block, block), block)
        part = jnp.dot(
            attended, wb[:, :, cols].reshape(NY * rows, block),
            preferred_element_type=jnp.float32,
        ).reshape(2, out_rows, block)
        ps[:, cols] = part[1].astype(jnp.bfloat16)
        hand_over(i).start()
        pf[:, cols] = part[0]
        return carry

    lax.fori_loop(0, 4, project, 0)

    def end_send(i, carry):
        pass_on(i).wait_send()
        return carry

    lax.fori_loop(1, 2 * NY, end_send, 0)
    def finish(i, carry):
        cols = pl.ds(pl.multiple_of(i * block, block), block)
        hand_over(i).wait_recv()
        out_ref[:, cols] = (
            pf[:, cols] + pr[:, cols].astype(jnp.float32)
        ).astype(out_ref.dtype)
        return carry

    lax.fori_loop(0, 4, finish, 0)
    for i in range(4):
        hand_over(i).wait_send()


def on_device(queries, keys, values, frame_mask, out_weight):
    rows = queries.shape[0]
    width = out_weight.shape[1]
    out_rows = rows // (2 * NY)
    hbm_spec = pl.BlockSpec(memory_space=pltpu.HBM)
    dma = pltpu.SemaphoreType.DMA
    bf16, f32 = jnp.bfloat16, jnp.float32
    return pl.pallas_call(
        kernel,
        out_shape=jax.ShapeDtypeStruct((out_rows, width), bf16),
        in_specs=[hbm_spec] * 5,
        out_specs=pl.BlockSpec(memory_space=pltpu.VMEM),
        scratch_shapes=[
            pltpu.SMEM(frame_mask.shape, frame_mask.dtype),
            pltpu.VMEM((2, rows, HD), bf16),
            pltpu.VMEM((2, NZ, 2, 2, rows, HD), bf16),
            pltpu.VMEM((NY, rows, width), bf16),
            pltpu.VMEM((2, rows, 2 * HD), f32),
            pltpu.VMEM((2, rows, HD), f32),
            pltpu.VMEM((2, NY, 2, out_rows, HD), bf16),
            pltpu.VMEM((NY, 2, 2, out_rows, HD), bf16),
            pltpu.VMEM((out_rows, width), f32),
            pltpu.VMEM((out_rows, width), bf16),
            pltpu.VMEM((out_rows, width), bf16),
            dma((5,)),
            dma((3,)), dma((3,)),
            dma((2, 2, 4)), dma((2, 2, 4)),
            dma((2, NZ)), dma((2, NZ)),
            dma((2, 2)), dma((2, 2)),
            dma((6,)), dma((6,)),
            dma((6,)), dma((6,)),
            dma((2 * NY,)), dma((2 * NY,)),
            dma((4,)), dma((4,)),
        ],
        compiler_params=pltpu.CompilerParams(
            collective_id=0, has_side_effects=True, vmem_limit_bytes=55040 * 1024
        ),
        cost_estimate=pl.CostEstimate(
            flops=3 * 10**9, bytes_accessed=10 * 2**20, transcendentals=4 * 2**20
        ),
    )(queries, keys, values, frame_mask, out_weight)


def solution(mesh):
    return jax.shard_map(
        on_device,
        mesh=mesh,
        in_specs=(P("ctx", "head"), P("ctx", "head"), P("ctx", "head"), P(), P("head", None)),
        out_specs=P(("ctx", "head"), None),
        check_vma=False,
    )
```

```python
import functools
import math

import jax
import jax.numpy as jnp
from jax import lax
from jax.experimental import pallas as pl
from jax.experimental.pallas import tpu as pltpu
from jax.sharding import PartitionSpec as P

HD = 128
FRAME_TOK = 128
NZ = 8
NY = 4
NEG_FILL = -1e30
LOG2E = 1.4426950408889634
MESH = pl.DeviceIdType.MESH


def kernel(
    q_hbm, k_hbm, v_hbm, mask_hbm, w_hbm, out_ref,
    mask, qb, kv, wb, acc, top, ob, ab, pf, ps, pr,
    local_sem, x_send, x_recv, f_send, z_send, z_recv, d_send, d_recv, e_send, e_recv,
    w_send, w_recv, c_send, c_recv, o_send, o_recv, p_send, p_recv,
):
    p = lax.axis_index("ctx")
    g = lax.axis_index("head")
    core = lax.rem(p, 2)
    zc = lax.rem(p, 2 * NZ)
    z = lax.div(zc, 2)
    xl = lax.div(p, 2 * NZ)
    y = lax.div(g, 2)
    xh = lax.rem(g, 2)
    rows = q_hbm.shape[0]
    half_cols = w_hbm.shape[1] // 2

    def device(xl_, z_, core_, y_, xh_):
        return ((xl_ * NZ + z_) * 2 + core_, y_ * 2 + xh_)

    def remote(src, dst, send, recv, target):
        return pltpu.make_async_remote_copy(
            src_ref=src, dst_ref=dst, send_sem=send, recv_sem=recv,
            device_id=target, device_id_type=MESH,
        )

    z_up, z_down = lax.rem(z + 1, NZ), lax.rem(z + NZ - 1, NZ)
    y_up, y_down = lax.rem(y + 1, NY), lax.rem(y + NY - 1, NY)
    sibling = device(xl, z, 1 - core, y, xh)
    partner = device(1 - xl, z, core, y, xh)
    up = device(xl, z_up, core, y, xh)
    down = device(xl, z_down, core, y, xh)
    w_up = device(xl, z, core, y_up, xh)
    w_down = device(xl, z, core, y_down, xh)

    def group_member(i):
        h = lax.rem(xl + lax.div(i, NY), 2)
        y_ = lax.rem(y + i, NY)
        return h, y_, device(h, z, core, y_, xh)

    own = pl.ds(pl.multiple_of(xl * HD, HD), HD)
    other = pl.ds(pl.multiple_of((1 - xl) * HD, HD), HD)
    w_cols = pl.ds(pl.multiple_of(core * half_cols, half_cols), half_cols)
    local = [
        pltpu.make_async_copy(k_hbm.at[:, own], kv.at[xl, z, core, 0], local_sem.at[0]),
        pltpu.make_async_copy(v_hbm.at[:, own], kv.at[xl, z, core, 1], local_sem.at[1]),
        pltpu.make_async_copy(q_hbm.at[:, own], qb.at[xl], local_sem.at[2]),
        pltpu.make_async_copy(w_hbm, wb.at[y], local_sem.at[3]),
        pltpu.make_async_copy(mask_hbm, mask, local_sem.at[4]),
    ]
    for copy in local:
        copy.start()

    barrier = pltpu.get_barrier_semaphore()

    def greet(i, carry):
        _, _, target = group_member(i)
        pl.semaphore_signal(barrier, inc=1, device_id=target, device_id_type=MESH)
        return carry

    across = device(1 - xl, z, core, y, 1 - xh)
    for target in (up, down, sibling, across):
        pl.semaphore_signal(barrier, inc=1, device_id=target, device_id_type=MESH)
    lax.fori_loop(1, 2 * NY, greet, 0)
    pl.semaphore_wait(barrier, 11)

    exchange = [
        remote(k_hbm.at[:, other], kv.at[xl, z, core, 0], x_send.at[0], x_recv.at[0], partner),
        remote(v_hbm.at[:, other], kv.at[xl, z, core, 1], x_send.at[1], x_recv.at[1], partner),
        remote(q_hbm.at[:, other], qb.at[xl], x_send.at[2], x_recv.at[2], partner),
    ]
    for copy in exchange[:2]:
        copy.start()

    def ring(direction, h, s):
        if direction == 0:
            unit = kv.at[h, lax.rem(z + NZ - s, NZ), core]
            target = up
        else:
            unit = kv.at[h, lax.rem(z + s, NZ), core]
            target = down
        return remote(
            unit, unit, z_send.at[direction, h, s], z_recv.at[direction, h, s], target
        )

    def ring_end(direction, h):
        piece = kv.at[h, lax.rem(z + (NZ - 3, 3)[direction], NZ), core, direction]
        return remote(
            piece, piece, z_send.at[direction, h, 3], z_recv.at[direction, h, 3],
            (up, down)[direction],
        )

    def share_end(kind, h):
        piece = kv.at[h, source(NZ - 1), core, kind]
        return remote(piece, piece, e_send.at[kind, h], e_recv.at[kind, h], sibling)

    def source(t):
        s = lax.div(t + 1, 2)
        return lax.rem(z + NZ + jnp.where(lax.rem(t, 2) == 1, -s, s), NZ)

    def first_ring(direction, i):
        return remote(
            (k_hbm, v_hbm)[i].at[:, own], kv.at[xl, z, core, i], f_send.at[direction, i],
            z_recv.at[direction, xl, 0], (up, down)[direction],
        )

    def share(h, t):
        unit = kv.at[h, source(t), core]
        return remote(unit, unit, d_send.at[h, t], d_recv.at[h, t], sibling)

    for direction in (0, 1):
        for i in (0, 1):
            first_ring(direction, i).start()
    local[0].wait()
    local[1].wait()
    share(xl, 0).start()

    w_half = rows // 2
    first, second = pl.ds(0, w_half), pl.ds(w_half, w_half)

    def w_own(i):
        part = (first, second, second, first)[i]
        return remote(
            w_hbm.at[part, w_cols], wb.at[y, part, w_cols], w_send.at[i], w_recv.at[i],
            (w_up, w_down, w_up, w_down)[i],
        )

    def w_forward(i):
        part = (first, second)[i]
        held = wb.at[(y_down, y_up)[i], part, w_cols]
        return remote(held, held, w_send.at[4 + i], w_recv.at[4 + i], (w_up, w_down)[i])

    def w_share(i):
        y_far = lax.rem(y + 2, NY)
        part = (first, second, second, first, first, second)[i]
        held = wb.at[(y_down, y_up, y_down, y_up, y_far, y_far)[i], part, w_cols]
        return remote(held, held, c_send.at[i], c_recv.at[i], sibling)

    for i in range(4):
        w_own(i).start()

    exchange[0].wait_recv()
    exchange[1].wait_recv()
    exchange[2].start()
    for direction in (0, 1):
        ring(direction, 1 - xl, 0).start()
    share(1 - xl, 0).start()

    acc[...] = jnp.zeros_like(acc)
    top[...] = jnp.full(top.shape, NEG_FILL, jnp.float32)

    scale = LOG2E / math.sqrt(HD)
    ones = jnp.ones((2 * rows, HD), jnp.bfloat16)

    def scores(q, half, src):
        k = kv[half, src, :, 0].reshape(2 * rows, HD)
        return lax.dot_general(
            q, k, (((1,), (1,)), ((), ())), preferred_element_type=jnp.float32
        )

    def absorb(h, parts):
        tiles = []
        for half, src in parts:
            s = scores(qb[h], half, src)
            for j in range(2 * rows // FRAME_TOK):
                key_frame = half * 4 * NZ + src * 4 + j
                fill = []
                for f in range(rows // FRAME_TOK):
                    allowed = mask[h * 4 * NZ + zc * 2 + f, key_frame]
                    fill.append(
                        jnp.full(
                            (FRAME_TOK, FRAME_TOK),
                            jnp.where(allowed > 0, 0.0, NEG_FILL),
                            jnp.float32,
                        )
                    )
                tiles.append(
                    s[:, j * FRAME_TOK:(j + 1) * FRAME_TOK] + jnp.concatenate(fill, axis=0)
                )
        best = functools.reduce(jnp.maximum, tiles)
        old_top = top[h]
        new_top = jnp.maximum(old_top, jnp.max(best, axis=1, keepdims=True))
        weights = [jnp.exp2((tile - new_top) * scale).astype(jnp.bfloat16) for tile in tiles]
        fade = jnp.exp2((old_top - new_top) * scale)
        total = acc[h] * jnp.concatenate([fade, fade], axis=1)
        per = 2 * rows // FRAME_TOK
        for i, (half, src) in enumerate(parts):
            v = kv[half, src, :, 1].reshape(2 * rows, HD)
            total += jnp.dot(
                jnp.concatenate(weights[i * per:(i + 1) * per], axis=1),
                jnp.concatenate([v, ones], axis=1),
                preferred_element_type=jnp.float32,
            )
        acc[h] = total
        top[h] = new_top

    def attend(*sources):
        absorb(0, [(0, src) for src in sources])
        absorb(1, [(half, src) for src in sources for half in (0, 1)])

    def step(u, carry):
        s, h = lax.div(u, 2) + 1, lax.rem(xl + u, 2)

        @pl.when(s < 4)
        def _():
            for direction in (0, 1):
                ring(direction, h, s - 1).wait_recv()

                @pl.when(s < 3)
                def _():
                    ring(direction, h, s).start()

                @pl.when(s == 3)
                def _():
                    ring_end(direction, h).start()

                share(h, 2 * s - 1 + direction).start()

        @pl.when(s == 4)
        def _():
            for direction in (0, 1):
                ring_end(direction, h).wait_recv()
                share_end(direction, h).start()

        @pl.when(u == 1)
        def _():
            local[2].wait()
            local[4].wait()
            exchange[2].wait_recv()

        @pl.when(u == 3)
        def _():
            for i in range(2):
                w_own(i).wait_recv()
                w_forward(i).start()
                w_share(i).start()

        @pl.when(u == 5)
        def _():
            for i in range(2, 4):
                w_own(i).wait_recv()
                w_share(i).start()

        @pl.when((u > 0) & (u < NZ))
        def _():
            for h_ in (0, 1):
                share(h_, u - 1).wait_recv()

        @pl.when(u == NZ)
        def _():
            for h_ in (0, 1):
                for kind in (0, 1):
                    share_end(kind, h_).wait_recv()

        @pl.when(u > 0)
        def _():
            attend(source(u - 1))

        return carry

    def pass_on(i):
        h, y_, target = group_member(i)
        return remote(
            ob.at[h, y_], ab.at[y, xl], o_send.at[i], o_recv.at[i], target
        )

    def end_pass(i, carry):
        pass_on(i).wait_recv()
        return carry

    lax.fori_loop(0, NZ + 1, step, 0)
    def conclude(h, carry):
        done = (acc[h, :, :HD] / acc[h, :, HD:]).astype(jnp.bfloat16).reshape(
            NY, 2, rows // (2 * NY), HD
        )
        for x_ in (0, 1):
            away = jnp.where(xh == x_, 0, 1)
            ob[jnp.where(xh == x_, h, 1 - h), :, away] = done[:, x_]
        return carry

    def start_pass(i, carry):
        pass_on(2 * NY - 1 - i).start()
        return carry

    lax.fori_loop(0, 2, conclude, 0)
    lax.fori_loop(0, 2 * NY - 1, start_pass, 0)
    ab[y, xl] = ob[xl, y]

    for i in range(2):
        w_forward(i).wait_recv()
        w_share(4 + i).start()

    for copy in exchange:
        copy.wait_send()
    for i in range(4):
        w_own(i).wait_send()
    for i in range(2):
        w_forward(i).wait_send()
    for i in range(6):
        w_share(i).wait_send()
        w_share(i).wait_recv()
    local[3].wait()

    def end_ring(s, carry):
        for direction in (0, 1):
            for h in (0, 1):

                @pl.when((s > 0) | (h != xl))
                def _():
                    ring(direction, h, s).wait_send()

        return carry

    def end_share(t, carry):
        share(0, t).wait_send()
        share(1, t).wait_send()
        return carry

    for direction in (0, 1):
        for i in (0, 1):
            first_ring(direction, i).wait_send()
    lax.fori_loop(0, 3, end_ring, 0)
    lax.fori_loop(0, NZ - 1, end_share, 0)
    for direction in (0, 1):
        for h in (0, 1):
            ring_end(direction, h).wait_send()
            share_end(direction, h).wait_send()
    lax.fori_loop(1, 2 * NY, end_pass, 0)

    attended = jnp.concatenate([ab[i, j].reshape(rows // NY, HD) for i in range(NY) for j in range(2)], axis=1)
    out_rows, width = out_ref.shape
    block = width // 4

    def hand_over(i):
        cols = pl.ds(pl.multiple_of(i * block, block), block)
        return remote(
            ps.at[:, cols], pr.at[:, cols], p_send.at[i], p_recv.at[i], across
        )

    def project(i, carry):
        cols = pl.ds(pl.multiple_of(i * block, block), block)
        part = jnp.dot(
            attended, wb[:, :, cols].reshape(NY * rows, block),
            preferred_element_type=jnp.float32,
        ).reshape(2, out_rows, block)
        ps[:, cols] = part[1].astype(jnp.bfloat16)
        hand_over(i).start()
        pf[:, cols] = part[0]
        return carry

    lax.fori_loop(0, 4, project, 0)

    def end_send(i, carry):
        pass_on(i).wait_send()
        return carry

    lax.fori_loop(1, 2 * NY, end_send, 0)
    def finish(i, carry):
        cols = pl.ds(pl.multiple_of(i * block, block), block)
        hand_over(i).wait_recv()
        out_ref[:, cols] = (
            pf[:, cols] + pr[:, cols].astype(jnp.float32)
        ).astype(out_ref.dtype)
        return carry

    lax.fori_loop(0, 4, finish, 0)
    for i in range(4):
        hand_over(i).wait_send()


def on_device(queries, keys, values, frame_mask, out_weight):
    rows = queries.shape[0]
    width = out_weight.shape[1]
    out_rows = rows // (2 * NY)
    hbm_spec = pl.BlockSpec(memory_space=pltpu.HBM)
    dma = pltpu.SemaphoreType.DMA
    bf16, f32 = jnp.bfloat16, jnp.float32
    return pl.pallas_call(
        kernel,
        out_shape=jax.ShapeDtypeStruct((out_rows, width), bf16),
        in_specs=[hbm_spec] * 5,
        out_specs=pl.BlockSpec(memory_space=pltpu.VMEM),
        scratch_shapes=[
            pltpu.SMEM(frame_mask.shape, frame_mask.dtype),
            pltpu.VMEM((2, rows, HD), bf16),
            pltpu.VMEM((2, NZ, 2, 2, rows, HD), bf16),
            pltpu.VMEM((NY, rows, width), bf16),
            pltpu.VMEM((2, rows, 2 * HD), f32),
            pltpu.VMEM((2, rows, HD), f32),
            pltpu.VMEM((2, NY, 2, out_rows, HD), bf16),
            pltpu.VMEM((NY, 2, 2, out_rows, HD), bf16),
            pltpu.VMEM((out_rows, width), f32),
            pltpu.VMEM((out_rows, width), bf16),
            pltpu.VMEM((out_rows, width), bf16),
            dma((5,)),
            dma((3,)), dma((3,)),
            dma((2, 2)), dma((2, 2, 4)), dma((2, 2, 4)),
            dma((2, NZ)), dma((2, NZ)),
            dma((2, 2)), dma((2, 2)),
            dma((6,)), dma((6,)),
            dma((6,)), dma((6,)),
            dma((2 * NY,)), dma((2 * NY,)),
            dma((4,)), dma((4,)),
        ],
        compiler_params=pltpu.CompilerParams(
            collective_id=0, has_side_effects=True, vmem_limit_bytes=55040 * 1024
        ),
        cost_estimate=pl.CostEstimate(
            flops=3 * 10**9, bytes_accessed=10 * 2**20, transcendentals=4 * 2**20
        ),
    )(queries, keys, values, frame_mask, out_weight)


def solution(mesh):
    return jax.shard_map(
        on_device,
        mesh=mesh,
        in_specs=(P("ctx", "head"), P("ctx", "head"), P("ctx", "head"), P(), P("head", None)),
        out_specs=P(("ctx", "head"), None),
        check_vma=False,
    )
```
